128 devices in a mesh: row: 16 (over z_lo, x, core), col: 8 (over z_hi, y).
Axes of the slice: x: 4, y: 4, z: 4 (z_hi: 2, z_lo: 2; z = z_hi * 2 + z_lo), core: 2. Of those that a mesh axis runs over, the one named last changes fastest.
Arguments:
- features: bfloat16 [65536, 256], P(('row', 'col')), may hold values from -6 to 6
- tile_edge_weights: bfloat16 [16, 8, 736, 128, 128], P('row', 'col'), as said below
- slot_block_row: int32 [16, 8, 736], P('row', 'col'), may hold values from 0 to 32, as said below
- slot_block_column: int32 [16, 8, 736], P('row', 'col'), may hold values from 0 to 63, as said below
- degree: int32 [65536], P(('row', 'col')), may hold values from 14 to 56
- w_self: bfloat16 [256, 256], replicated, may hold values from -0.375 to 0.375
- w_neigh: bfloat16 [256, 256], replicated, may hold values from -0.375 to 0.375
Outputs:
- updated: bfloat16 [65536, 256], P(('row', 'col'))
The draws below stay inside these ranges and needn't reach their ends.
Inputs may be any that keep to these rules, and one draw needn't show every extreme that they name: `slot_block_row`: block slot rows: live slots come first in each tile; dead slots hold 4 * 8. Each tile has between 184 and 736 live slots, distinct (row, column) pairs; some tile is full and some tile has 184. `slot_block_column`: dead slots hold the largest column. `tile_edge_weights`: each block holds about 40 nonzero edge weights, the rest zero.
All inputs are finite; a program needn't handle non-finite values.
Results may differ from the reference program's by a relative error of at most 0.0034.
Values may be sent and summed in bfloat16 or wider, within the bound.
A program may use at most 128 MiB of HBM per device.

```python
import jax
import jax.numpy as jnp
from jax import lax

D = 256
BS = 128
NNZ_BLK = 40
BLK_PIECE = 4
NODES = 65536
NBLK = 736
DEG = 28
N_ROW = 16
N_COL = 8


def block_layout(key):
    tiles = N_ROW * N_COL
    col_span = N_ROW * BLK_PIECE
    spots = N_COL * BLK_PIECE * col_span
    keys = jax.random.split(key, tiles + 1)
    perms = jax.vmap(lambda k: jax.random.permutation(k, spots)[:NBLK])(keys[:tiles])
    counts = jax.random.randint(keys[tiles], (tiles,), NBLK // 4, NBLK + 1)
    chosen = jax.random.permutation(jax.random.fold_in(keys[tiles], 1), tiles)
    counts = counts.at[chosen[0]].set(NBLK).at[chosen[1]].set(NBLK // 4)
    slots = jnp.arange(NBLK, dtype=jnp.int32)
    live = slots[None, :] < counts[:, None]
    row_indices = jnp.where(live, perms // col_span, N_COL * BLK_PIECE)
    column_indices = jnp.where(live, perms % col_span, col_span - 1)
    return (row_indices.reshape(N_ROW, N_COL, NBLK).astype(jnp.int32), column_indices.reshape(N_ROW, N_COL, NBLK).astype(jnp.int32))


def draw_slot_block_row(key, part):
    row_indices, column_indices = block_layout(key)
    return row_indices


def draw_slot_block_column(key, part):
    row_indices, column_indices = block_layout(key)
    return column_indices


def draw_tile_edge_weights(key, part):
    key = jax.random.fold_in(key, 7)
    share = NNZ_BLK / (BS * BS)
    draws = jax.random.uniform(key, (N_ROW, N_COL, NBLK, BS, BS), jnp.float32)
    level = 2.0 * draws / share - 1.0
    spread = 5.2 * level
    return jnp.where(draws < share, spread, 0.0).astype(jnp.bfloat16)


def place_ends(drawn, stream_key, smallest, largest):
    place = [jax.random.randint(jax.random.fold_in(stream_key, axis), (), 0, length) for axis, length in enumerate(drawn.shape)]
    longest = drawn.shape.index(max(drawn.shape))
    neighbour = place[:longest] + [(place[longest] + 1) % drawn.shape[longest]] + place[longest + 1:]
    return drawn.at[tuple(place)].set(smallest).at[tuple(neighbour)].set(largest)


def shard_levels(own_key, dims, shards, least, top_value):
    gain = 1.0
    for dim, blocks in shards:
        steps = jax.random.uniform(jax.random.fold_in(jax.random.fold_in(own_key, 6), dim), (blocks,), jnp.float32, least / len(shards), top_value / len(shards))
        gain = gain * jnp.repeat(jnp.exp(steps), dims[dim] // blocks).reshape((-1,) + (1,) * (len(dims) - 1 - dim))
    return gain


def gaussian(key, extent, deviation, bound, cuts=(), kind=jnp.bfloat16):
    drawn = jax.random.normal(key, extent, jnp.float32) * deviation
    if len(cuts) > 0:
        drawn = shard_levels(key, extent, cuts, -0.22, 0.18) * drawn
    return jnp.clip(drawn, min=-bound, max=bound).astype(kind)


def setup_inputs(seed: int = 0) -> dict:
    key_of = jax.random.split(jax.random.key(seed), 8)
    return {
        "features": gaussian(key_of[0], (NODES, D), 1.0, 6.0, ((0, 128),)),
        "tile_edge_weights": draw_tile_edge_weights(jax.random.fold_in(key_of[7], 71), 0),
        "slot_block_row": draw_slot_block_row(jax.random.fold_in(key_of[7], 71), 0),
        "slot_block_column": draw_slot_block_column(jax.random.fold_in(key_of[7], 71), 0),
        "degree": place_ends(jax.random.randint(key_of[4], (NODES,), DEG // 2, 2 * DEG + 1), jax.random.fold_in(key_of[4], 1), DEG // 2, 2 * DEG).astype(jnp.int32),
        "w_self": gaussian(key_of[5], (D, D), D ** -0.5, 0.375),
        "w_neigh": gaussian(key_of[6], (D, D), D ** -0.5, 0.375),
    }


def reference(features, tile_edge_weights, slot_block_row, slot_block_column, degree, w_self, w_neigh):
    out_blocks = N_COL * BLK_PIECE
    pieces = features.reshape(N_ROW, N_COL, BLK_PIECE * BS, D)

    def row_group(i):
        def tile_sum(acc, j):
            group = lax.dynamic_index_in_dim(pieces, j, 1, keepdims=False).reshape(N_ROW * BLK_PIECE, BS, D)
            row_indices = slot_block_row[i, j]
            column_indices = slot_block_column[i, j]
            vals = tile_edge_weights[i, j].astype(jnp.float32)
            picked = group[column_indices].astype(jnp.float32)
            prod = jnp.einsum('sij,sjd->sid', vals, picked)
            summed = jax.ops.segment_sum(prod, row_indices, num_segments=out_blocks + 1)[:out_blocks]
            return acc + summed, None
        start = jnp.zeros((out_blocks, BS, D), jnp.float32)
        total, _ = lax.scan(tile_sum, start, jnp.arange(N_COL, dtype=jnp.int32))
        return total

    neighbour_sum = lax.map(row_group, jnp.arange(N_ROW, dtype=jnp.int32)).reshape(NODES, D)
    neighbour_mean = (neighbour_sum / degree.astype(jnp.float32)[:, None]).astype(jnp.bfloat16)
    own = jnp.dot(features, w_self, preferred_element_type=jnp.float32)
    other = jnp.dot(neighbour_mean, w_neigh, preferred_element_type=jnp.float32)
    return jax.nn.relu(own + other).astype(jnp.bfloat16)
```

```python
import functools

import jax
import jax.numpy as jnp
from jax import lax
from jax.experimental import pallas as pl
from jax.experimental.pallas import tpu as pltpu
from jax.sharding import PartitionSpec as P

MESH = pl.DeviceIdType.MESH
BS = 128
D = 256
PIECE = 512
NBLK = 736
LANES = 768
ROW_BLOCKS = 32
COL_BLOCKS = 64
CHUNK = 16


def row_at(i, dz, dx, dc):
    return ((i // 8 + dz) % 2) * 8 + ((i // 2 + dx + 4) % 4) * 2 + (i + dc) % 2


def col_at(j, dz, dy):
    return ((j // 4 + dz) % 2) * 4 + (j + dy + 4) % 4


def gather_plan():
    half, quarter = PIECE // 2, PIECE // 4
    upper, lower = (0, half), (half, half)
    right, left, over, core = (0, 1, 0), (0, -1, 0), (1, 0, 0), (0, 0, 1)
    return [
        (None, [
            ("a1", (0, 0), *upper, right), ("a2", (0, 0), *upper, left),
            ("bz", (0, 0), *lower, over), ("az", (0, 0), *upper, over),
            ("b1", (0, 0), *lower, right), ("b2", (0, 0), *lower, left),
            ("s0", (0, 0), 0, PIECE, core)]),
        ("a1", [("az1", (0, -1), *upper, over), ("a3", (0, -1), 0, quarter, right),
                ("s1", (0, -1), *upper, core)]),
        ("a2", [("az2", (0, 1), *upper, over), ("a4", (0, 1), quarter, quarter, left),
                ("s2", (0, 1), *upper, core)]),
        ("bz", [("zb1", (1, 0), *lower, right), ("zb2", (1, 0), *lower, left),
                ("s3", (1, 0), *lower, core)]),
        ("b1", [("b3", (0, -1), half, quarter, right), ("s4", (0, -1), *lower, core)]),
        ("b2", [("b4", (0, 1), half + quarter, quarter, left), ("s5", (0, 1), *lower, core)]),
        ("az", [("s6", (1, 0), *upper, core)]),
        ("a3", [("az3", (0, 2), 0, quarter, over), ("s7", (0, 2), 0, quarter, core)]),
        ("a4", [("az4", (0, 2), quarter, quarter, over), ("s8", (0, 2), quarter, quarter, core)]),
        ("zb1", [("zb3", (1, -1), half, quarter, right), ("s9", (1, -1), *lower, core)]),
        ("zb2", [("zb4", (1, 1), half + quarter, quarter, left), ("s10", (1, 1), *lower, core)]),
        ("az1", [("s11", (1, -1), *upper, core)]),
        ("az2", [("s12", (1, 1), *upper, core)]),
        ("b3", [("s13", (0, 2), half, quarter, core)]),
        ("b4", [("s14", (0, 2), half + quarter, quarter, core)]),
        ("zb3", [("s15", (1, 2), half, quarter, core)]),
        ("zb4", [("s16", (1, 2), half + quarter, quarter, core)]),
        ("az3", [("s17", (1, 2), 0, quarter, core)]),
        ("az4", [("s18", (1, 2), quarter, quarter, core)]),
    ]


PLAN = gather_plan()
SENDS = {copy[0]: copy for _, copies in PLAN for copy in copies}
PLACE = {name: k for k, name in enumerate(SENDS)}


def step_offset(k):
    m = k // 2
    return 1 - k % 2, (2 + m + m * (m - 1) // 2) % 4


def kernel(
    rows_ref, cols_ref, degree_ref, w_self_ref, w_neigh_ref, x_hbm, a_hbm, out_ref,
    gathered, blocks, table_v, table_s, own, acc, sent, got, slots,
    load_sem, x_sem, table_sem, g_send, g_recv, c_send, c_recv,
):
    i, j = lax.axis_index("row"), lax.axis_index("col")

    load = pltpu.make_async_copy(a_hbm, blocks.at[pl.ds(1, NBLK)], load_sem)
    load.start()
    x_load = pltpu.make_async_copy(x_hbm, gathered.at[i], x_sem)
    x_load.start()

    barrier = pltpu.get_barrier_semaphore()
    near = [(0, 1, 0), (0, -1, 0), (1, 0, 0), (0, 0, 1)]
    for offset in near:
        pl.semaphore_signal(barrier, inc=1, device_id=(row_at(i, *offset), j), device_id_type=MESH)
    for k in range(7):
        pl.semaphore_signal(
            barrier, inc=1, device_id=(i, col_at(j, *step_offset(k))), device_id_type=MESH)
    pl.semaphore_wait(barrier, len(near) + 7)

    def gather_copy(name, arriving=False):
        _, (dz, dx), first, count, target = SENDS[name]
        if arriving:
            place = row_at(i, dz - target[0], dx - target[1], -target[2])
        else:
            place = row_at(i, dz, dx, 0)
        region = gathered.at[place, pl.ds(first, count)]
        source = region
        if not arriving and (dz, dx) == (0, 0):
            source = x_hbm.at[pl.ds(first, count)]
        return pltpu.make_async_remote_copy(
            src_ref=source, dst_ref=region,
            send_sem=g_send.at[PLACE[name]], recv_sem=g_recv.at[PLACE[name]],
            device_id=(row_at(i, *target), j), device_id_type=MESH)

    waited = set()

    def gather_steps(steps):
        for name, copies in steps:
            if name is not None:
                gather_copy(name, arriving=True).wait_recv()
                waited.add(name)
            for copy in copies:
                gather_copy(copy[0]).start()

    gather_steps(PLAN[:1])

    slots[...] = jnp.full_like(slots, -1)
    slots[0:1, 0:NBLK] = rows_ref[...]
    slots[1:2, 0:NBLK] = cols_ref[...]
    place = lax.broadcasted_iota(jnp.int32, (COL_BLOCKS, LANES), 1) + 1
    here = lax.broadcasted_iota(jnp.int32, (COL_BLOCKS, LANES), 0) == slots[1:2, :]
    in_row = lax.broadcasted_iota(jnp.int32, (ROW_BLOCKS, LANES), 0) == slots[0:1, :]
    in_row = in_row.astype(jnp.float32).astype(jnp.bfloat16)
    high = jnp.where(here, place >> 5, 0).astype(jnp.float32).astype(jnp.bfloat16)
    low = jnp.where(here, place & 31, 0).astype(jnp.float32).astype(jnp.bfloat16)
    dims = (((1,), (1,)), ((), ()))
    found = 32.0 * lax.dot_general(in_row, high, dims, preferred_element_type=jnp.float32)
    found += lax.dot_general(in_row, low, dims, preferred_element_type=jnp.float32)
    table_v[...] = jnp.clip(found.astype(jnp.int32), 0, NBLK)
    table_copy = pltpu.make_async_copy(table_v, table_s, table_sem)
    table_copy.start()
    blocks[0] = jnp.zeros((BS, BS), jnp.bfloat16)

    gather_steps(PLAN[1:3])
    x_load.wait()
    gather_steps(PLAN[3:4])
    for b in range(4):
        rows = pl.ds(b * BS, BS)
        own[rows, :] = jnp.dot(
            gathered[i, rows, :], w_self_ref[...], preferred_element_type=jnp.float32)
    gather_steps(PLAN[4:])
    table_copy.wait()
    for name in SENDS:
        if name not in waited:
            gather_copy(name, arriving=True).wait_recv()
    load.wait()

    def piece_sum(piece):
        acc[...] = jnp.zeros_like(acc)

        def chunk(c, _):
            for p in range(0, CHUNK, 2):
                first = c * CHUNK + p
                block = first % 4
                x = gathered[first // 4, pl.ds(pl.multiple_of(block * BS, 2 * BS), 2 * BS), :]
                for b in range(4):
                    r = piece * 4 + b
                    a = jnp.concatenate(
                        [blocks[table_s[r, first]], blocks[table_s[r, first + 1]]], axis=1)
                    acc[b] += jnp.dot(a, x, preferred_element_type=jnp.float32)
            return 0

        lax.fori_loop(0, COL_BLOCKS // CHUNK, chunk, 0)

    def piece_copy(k):
        return pltpu.make_async_remote_copy(
            src_ref=sent.at[k], dst_ref=got.at[k], send_sem=c_send.at[k], recv_sem=c_recv.at[k],
            device_id=(i, col_at(j, *step_offset(k))), device_id_type=MESH)

    def send_step(k, _):
        piece_sum(col_at(j, *step_offset(k)))
        for b in range(4):
            sent[k, pl.ds(b * BS, BS), :] = acc[b].astype(jnp.bfloat16)
        piece_copy(k).start()
        return 0

    lax.fori_loop(0, 7, send_step, 0)
    piece_sum(j)
    for k in range(7):
        piece_copy(k).wait_recv()
    for b in range(4):
        rows = pl.ds(b * BS, BS)
        total = acc[b]
        for k in range(7):
            total += got[k, rows, :].astype(jnp.float32)
        degree = jnp.broadcast_to(degree_ref[b:b + 1, :].astype(jnp.float32), (BS, BS)).T
        degree = jnp.concatenate([degree, degree], axis=1)
        mean = (total / degree).astype(jnp.bfloat16)
        new = own[rows, :] + jnp.dot(mean, w_neigh_ref[...], preferred_element_type=jnp.float32)
        out_ref[rows, :] = jnp.maximum(new, 0.0).astype(jnp.bfloat16)
    for k in range(7):
        piece_copy(k).wait_send()
    for name in SENDS:
        gather_copy(name).wait_send()


def per_device(features, weights, slot_row, slot_column, degree, w_self, w_neigh):
    vmem = pl.BlockSpec(memory_space=pltpu.VMEM)
    hbm = pl.BlockSpec(memory_space=pl.ANY)
    count = len(SENDS)
    return pl.pallas_call(
        kernel,
        out_shape=jax.ShapeDtypeStruct((PIECE, D), jnp.bfloat16),
        in_specs=[vmem] * 5 + [hbm] * 2,
        out_specs=vmem,
        scratch_shapes=[
            pltpu.VMEM((16, PIECE, D), jnp.bfloat16),
            pltpu.VMEM((NBLK + 1, BS, BS), jnp.bfloat16),
            pltpu.VMEM((ROW_BLOCKS, COL_BLOCKS), jnp.int32),
            pltpu.SMEM((ROW_BLOCKS, COL_BLOCKS), jnp.int32),
            pltpu.VMEM((PIECE, D), jnp.float32),
            pltpu.VMEM((4, BS, D), jnp.float32),
            pltpu.VMEM((7, PIECE, D), jnp.bfloat16),
            pltpu.VMEM((7, PIECE, D), jnp.bfloat16),
            pltpu.VMEM((8, LANES), jnp.int32),
            pltpu.SemaphoreType.DMA,
            pltpu.SemaphoreType.DMA,
            pltpu.SemaphoreType.DMA,
            pltpu.SemaphoreType.DMA((count,)),
            pltpu.SemaphoreType.DMA((count,)),
            pltpu.SemaphoreType.DMA((7,)),
            pltpu.SemaphoreType.DMA((7,)),
        ],
        compiler_params=pltpu.CompilerParams(
            collective_id=0, has_side_effects=True, vmem_limit_bytes=52 * 2**20),
        name="sage_layer",
    )(
        slot_row.reshape(1, NBLK), slot_column.reshape(1, NBLK), degree.reshape(4, BS),
        w_self, w_neigh, features, weights.reshape(NBLK, BS, BS),
    )


def solution(mesh):
    in_specs = (
        P(("row", "col"), None),
        P("row", "col", None, None, None),
        P("row", "col", None),
        P("row", "col", None),
        P(("row", "col")),
        P(),
        P(),
    )
    return jax.shard_map(
        per_device, mesh=mesh, in_specs=in_specs, out_specs=P(("row", "col"), None), check_vma=False)
```

```python
import jax
import jax.numpy as jnp
from jax import lax
from jax.experimental import pallas as pl
from jax.experimental.pallas import tpu as pltpu
from jax.sharding import PartitionSpec as P

MESH = pl.DeviceIdType.MESH
BS = 128
D = 256
PIECE = 512
NBLK = 736
LANES = 768
ROW_BLOCKS = 32
COL_BLOCKS = 64


def row_at(i, dz, dx, dc):
    return ((i // 8 + dz) % 2) * 8 + ((i // 2 + dx + 4) % 4) * 2 + (i + dc) % 2


def col_at(j, dz, dy):
    return ((j // 4 + dz) % 2) * 4 + (j + dy + 4) % 4


def gather_plan():
    half, quarter = PIECE // 2, PIECE // 4
    upper, lower = (0, half), (half, half)
    right, left, over, core = (0, 1, 0), (0, -1, 0), (1, 0, 0), (0, 0, 1)
    return [
        (None, [
            ("a1", (0, 0), *upper, right), ("a2", (0, 0), *upper, left),
            ("bz", (0, 0), *lower, over), ("az", (0, 0), *upper, over),
            ("b1", (0, 0), *lower, right), ("b2", (0, 0), *lower, left),
            ("s0", (0, 0), 0, PIECE, core)]),
        ("a1", [("az1", (0, -1), *upper, over), ("a3", (0, -1), 0, quarter, right),
                ("s1", (0, -1), *upper, core)]),
        ("a2", [("az2", (0, 1), *upper, over), ("a4", (0, 1), quarter, quarter, left),
                ("s2", (0, 1), *upper, core)]),
        ("bz", [("zb1", (1, 0), *lower, right), ("zb2", (1, 0), *lower, left),
                ("s3", (1, 0), *lower, core)]),
        ("b1", [("b3", (0, -1), half, quarter, right), ("s4", (0, -1), *lower, core)]),
        ("b2", [("b4", (0, 1), half + quarter, quarter, left), ("s5", (0, 1), *lower, core)]),
        ("az", [("s6", (1, 0), *upper, core)]),
        ("a3", [("az3", (0, 2), 0, quarter, over), ("s7", (0, 2), 0, quarter, core)]),
        ("a4", [("az4", (0, 2), quarter, quarter, over), ("s8", (0, 2), quarter, quarter, core)]),
        ("zb1", [("zb3", (1, -1), half, quarter, right), ("s9", (1, -1), *lower, core)]),
        ("zb2", [("zb4", (1, 1), half + quarter, quarter, left), ("s10", (1, 1), *lower, core)]),
        ("az1", [("s11", (1, -1), *upper, core)]),
        ("az2", [("s12", (1, 1), *upper, core)]),
        ("b3", [("s13", (0, 2), half, quarter, core)]),
        ("b4", [("s14", (0, 2), half + quarter, quarter, core)]),
        ("zb3", [("s15", (1, 2), half, quarter, core)]),
        ("zb4", [("s16", (1, 2), half + quarter, quarter, core)]),
        ("az3", [("s17", (1, 2), 0, quarter, core)]),
        ("az4", [("s18", (1, 2), quarter, quarter, core)]),
    ]


PLAN = gather_plan()
SENDS = {copy[0]: copy for _, copies in PLAN for copy in copies}
PLACE = {name: k for k, name in enumerate(SENDS)}


STEPS = [(1, 2), (1, -1), (1, 1), (0, 2), (1, 0), (0, -1), (0, 1), (0, 0)]
EARLY = [(0, 0), (0, 1), (0, -1)]
LATE = [(1, 0), (0, 2), (1, 1), (1, -1), (1, 2)]
Z_ROWS = 256
Y_HALF = Z_ROWS + (PIECE - Z_ROWS) // 2
OVER, RIGHT, LEFT = (1, 0), (0, 1), (0, -1)
PARTS = {
    "z2": ((1, 2), 0, Z_ROWS, OVER), "zl": ((1, -1), 0, Z_ROWS, OVER),
    "zr": ((1, 1), 0, Z_ROWS, OVER),
    "o2r": ((1, 2), Z_ROWS, Y_HALF - Z_ROWS, RIGHT), "o2l": ((1, 2), Y_HALF, PIECE - Y_HALF, LEFT),
    "o1r": ((1, 1), Z_ROWS, PIECE - Z_ROWS, RIGHT), "o1l": ((1, -1), Z_ROWS, PIECE - Z_ROWS, LEFT),
    "n2r": ((0, 2), 0, PIECE // 2, RIGHT), "n2l": ((0, 2), PIECE // 2, PIECE // 2, LEFT),
    "n1r": ((0, 1), 0, PIECE, RIGHT), "n1l": ((0, -1), 0, PIECE, LEFT),
    "o0": ((1, 0), 0, PIECE, OVER),
}
PART_PLACE = {name: k for k, name in enumerate(PARTS)}
PART_START = {}
PART_ROWS = 0
for _name, _part in PARTS.items():
    PART_START[_name] = PART_ROWS
    PART_ROWS += _part[2]


def step_piece(j, k):
    dz, dy = 0, 0
    for step, (z, y) in enumerate(STEPS):
        dz = jnp.where(k == step, z, dz)
        dy = jnp.where(k == step, y, dy)
    return col_at(j, dz, dy)


def kernel(
    rows_hbm, cols_hbm, degree_hbm, w_self_hbm, w_neigh_hbm, x_hbm, a_hbm, out_ref,
    gathered, blocks, table_v, table_s, own, acc, sent, got, slots,
    rows_v, cols_v, degree_v, w_self, w_neigh,
    load_sem, table_sem, g_send, g_recv, c_send, c_recv,
):
    i, j = lax.axis_index("row"), lax.axis_index("col")

    loads = [
        pltpu.make_async_copy(source, target, load_sem.at[k])
        for k, (source, target) in enumerate([
            (rows_hbm, rows_v), (cols_hbm, cols_v), (x_hbm, gathered.at[i]), (w_self_hbm, w_self),
            (a_hbm, blocks.at[pl.ds(1, NBLK)]), (degree_hbm, degree_v), (w_neigh_hbm, w_neigh)])
    ]
    for load in loads:
        load.start()

    barrier = pltpu.get_barrier_semaphore()
    near = [(0, 1, 0), (0, -1, 0), (1, 0, 0), (0, 0, 1)]
    for offset in near:
        pl.semaphore_signal(barrier, inc=1, device_id=(row_at(i, *offset), j), device_id_type=MESH)
    for offset in (OVER, RIGHT, LEFT):
        pl.semaphore_signal(barrier, inc=1, device_id=(i, col_at(j, *offset)), device_id_type=MESH)
    pl.semaphore_wait(barrier, len(near) + 3)

    def gather_copy(name, arriving=False):
        _, (dz, dx), first, count, target = SENDS[name]
        if arriving:
            place = row_at(i, dz - target[0], dx - target[1], -target[2])
        else:
            place = row_at(i, dz, dx, 0)
        region = gathered.at[place, pl.ds(first, count)]
        source = region
        if not arriving and (dz, dx) == (0, 0):
            source = x_hbm.at[pl.ds(first, count)]
        return pltpu.make_async_remote_copy(
            src_ref=source, dst_ref=region,
            send_sem=g_send.at[PLACE[name]], recv_sem=g_recv.at[PLACE[name]],
            device_id=(row_at(i, *target), j), device_id_type=MESH)

    waited = set()

    def gather_wait(*names):
        for name in names:
            gather_copy(name, arriving=True).wait_recv()
            waited.add(name)

    def gather_steps(*names):
        for name, copies in PLAN:
            if name in names:
                if name is not None:
                    gather_wait(name)
                for copy in copies:
                    gather_copy(copy[0]).start()

    gather_steps(None)

    loads[0].wait()
    loads[1].wait()
    slots[...] = jnp.full_like(slots, -1)
    slots[0:1, 0:NBLK] = rows_v[...]
    slots[1:2, 0:NBLK] = cols_v[...]
    place = lax.broadcasted_iota(jnp.int32, (COL_BLOCKS, LANES), 1) + 1
    here = lax.broadcasted_iota(jnp.int32, (COL_BLOCKS, LANES), 0) == slots[1:2, :]
    in_row = lax.broadcasted_iota(jnp.int32, (ROW_BLOCKS, LANES), 0) == slots[0:1, :]
    in_row = in_row.astype(jnp.float32).astype(jnp.bfloat16)
    high = jnp.where(here, place >> 5, 0).astype(jnp.float32).astype(jnp.bfloat16)
    low = jnp.where(here, place & 31, 0).astype(jnp.float32).astype(jnp.bfloat16)
    dims = (((1,), (1,)), ((), ()))
    found = 32.0 * lax.dot_general(in_row, high, dims, preferred_element_type=jnp.float32)
    found += lax.dot_general(in_row, low, dims, preferred_element_type=jnp.float32)
    table_v[...] = jnp.clip(found.astype(jnp.int32), 0, NBLK)
    table_copy = pltpu.make_async_copy(table_v, table_s, table_sem)
    table_copy.start()
    blocks[0] = jnp.zeros((BS, BS), jnp.bfloat16)

    def clear(k, _):
        acc[k] = jnp.zeros((PIECE, D), jnp.float32)
        return 0

    lax.fori_loop(0, 8, clear, 0)
    loads[2].wait()
    loads[3].wait()
    for b in range(4):
        rows = pl.ds(b * BS, BS)
        own[rows, :] = jnp.dot(
            gathered[i, rows, :], w_self[...], preferred_element_type=jnp.float32)
    gather_steps("a1", "a2", "bz", "b1", "b2", "az")
    table_copy.wait()
    gather_wait("s0", "s1", "s2", "s4", "s5")
    loads[4].wait()

    def add_products(k, chips):
        piece = step_piece(j, k)
        for b in range(4):
            total = None
            for dz, dx in chips:
                chip = ((i // 8 + dz) % 2) * 4 + (i // 2 + dx + 4) % 4
                for c in range(0, 8, 2):
                    x = gathered[2 * chip + c // 4, pl.ds((c % 4) * BS, 2 * BS), :]
                    slot = [table_s[piece * 4 + b, chip * 8 + c + d] for d in range(2)]
                    a = jnp.concatenate([blocks[slot[0]], blocks[slot[1]]], axis=1)
                    term = jnp.dot(a, x, preferred_element_type=jnp.float32)
                    total = term if total is None else total + term
            acc[piece, pl.ds(b * BS, BS), :] += total

    def part_copy(name):
        piece, first, count, target = PARTS[name]
        return pltpu.make_async_remote_copy(
            src_ref=sent.at[STEPS.index(piece), pl.ds(first, count)],
            dst_ref=got.at[pl.ds(PART_START[name], count)],
            send_sem=c_send.at[PART_PLACE[name]], recv_sem=c_recv.at[PART_PLACE[name]],
            device_id=(i, col_at(j, *target)), device_id_type=MESH)

    def arrived(name, first, count):
        start = PART_START[name] + first - PARTS[name][1]
        return got[pl.ds(start, count), :].astype(jnp.float32)

    def finish(piece, terms, parts):
        k = STEPS.index(piece)
        for name in terms:
            part_copy(name).wait_recv()
        cuts = sorted({PARTS[n][1] for n in parts} | {PARTS[n][1] + PARTS[n][2] for n in parts}
                      | {PARTS[n][1] for n in terms} | {PARTS[n][1] + PARTS[n][2] for n in terms})
        low, high = PARTS[parts[0]][1], PARTS[parts[-1]][1] + PARTS[parts[-1]][2]
        cuts = [c for c in cuts if low <= c <= high]
        for first, last in zip(cuts, cuts[1:]):
            value = acc[col_at(j, *piece), pl.ds(first, last - first), :]
            for name in terms:
                if PARTS[name][1] <= first and last <= PARTS[name][1] + PARTS[name][2]:
                    value += arrived(name, first, last - first)
            sent[k, pl.ds(first, last - first), :] = value.astype(jnp.bfloat16)
        for name in parts:
            part_copy(name).start()

    def early_step(k, _):
        add_products(k, EARLY)
        for step, names in enumerate([
                ("a3", "a4"), ("zb1", "zb2"), ("az1", "az2"), ("b3", "b4"), ("zb3", "zb4"),
                ("az3", "az4")]):
            @pl.when(k == step)
            def _(names=names):
                gather_steps(*names)
        return 0

    lax.fori_loop(0, 8, early_step, 0)
    gather_wait(*[name for name in SENDS if name not in waited])

    actions = {
        0: [((1, 2), [], ["z2", "o2r", "o2l"])],
        1: [((1, -1), [], ["zl"]), ((1, -1), ["o2l"], ["o1l"])],
        2: [((1, 1), [], ["zr"]), ((1, 1), ["o2r"], ["o1r"])],
        4: [((0, 2), ["z2"], ["n2r", "n2l"])],
        5: [((1, 0), ["o1r", "o1l"], ["o0"])],
        6: [((0, -1), ["zl", "n2l"], ["n1l"])],
        7: [((0, 1), ["zr", "n2r"], ["n1r"])],
    }

    def late_step(k, _):
        add_products(k, LATE)
        for step, todo in actions.items():
            @pl.when(k == step)
            def _(todo=todo):
                for piece, terms, parts in todo:
                    finish(piece, terms, parts)
        return 0

    lax.fori_loop(0, 8, late_step, 0)
    loads[5].wait()
    loads[6].wait()
    for name in ("n1r", "n1l", "o0"):
        part_copy(name).wait_recv()
    for b in range(4):
        rows = pl.ds(b * BS, BS)
        total = acc[j, rows, :]
        for name in ("n1r", "n1l", "o0"):
            total += arrived(name, b * BS, BS)
        degree = jnp.broadcast_to(degree_v[b:b + 1, :].astype(jnp.float32), (BS, BS)).T
        degree = jnp.concatenate([degree, degree], axis=1)
        mean = (total / degree).astype(jnp.bfloat16)
        new = own[rows, :] + jnp.dot(mean, w_neigh[...], preferred_element_type=jnp.float32)
        out_ref[rows, :] = jnp.maximum(new, 0.0).astype(jnp.bfloat16)
    for name in PARTS:
        part_copy(name).wait_send()
    for name in SENDS:
        gather_copy(name).wait_send()


def per_device(features, weights, slot_row, slot_column, degree, w_self, w_neigh):
    hbm = pl.BlockSpec(memory_space=pltpu.HBM)
    count = len(SENDS)
    return pl.pallas_call(
        kernel,
        out_shape=jax.ShapeDtypeStruct((PIECE, D), jnp.bfloat16),
        in_specs=[hbm] * 7,
        out_specs=pl.BlockSpec(memory_space=pltpu.VMEM),
        scratch_shapes=[
            pltpu.VMEM((16, PIECE, D), jnp.bfloat16),
            pltpu.VMEM((NBLK + 1, BS, BS), jnp.bfloat16),
            pltpu.VMEM((ROW_BLOCKS, COL_BLOCKS), jnp.int32),
            pltpu.SMEM((ROW_BLOCKS, COL_BLOCKS), jnp.int32),
            pltpu.VMEM((PIECE, D), jnp.float32),
            pltpu.VMEM((8, PIECE, D), jnp.float32),
            pltpu.VMEM((7, PIECE, D), jnp.bfloat16),
            pltpu.VMEM((PART_ROWS, D), jnp.bfloat16),
            pltpu.VMEM((8, LANES), jnp.int32),
            pltpu.VMEM((1, NBLK), jnp.int32),
            pltpu.VMEM((1, NBLK), jnp.int32),
            pltpu.VMEM((4, BS), jnp.int32),
            pltpu.VMEM((D, D), jnp.bfloat16),
            pltpu.VMEM((D, D), jnp.bfloat16),
            pltpu.SemaphoreType.DMA((7,)),
            pltpu.SemaphoreType.DMA,
            pltpu.SemaphoreType.DMA((count,)),
            pltpu.SemaphoreType.DMA((count,)),
            pltpu.SemaphoreType.DMA((len(PARTS),)),
            pltpu.SemaphoreType.DMA((len(PARTS),)),
        ],
        compiler_params=pltpu.CompilerParams(
            collective_id=0, has_side_effects=True, vmem_limit_bytes=60 * 2**20),
        name="sage_layer",
    )(
        slot_row.reshape(1, NBLK), slot_column.reshape(1, NBLK), degree.reshape(4, BS),
        w_self, w_neigh, features, weights.reshape(NBLK, BS, BS),
    )


def solution(mesh):
    in_specs = (
        P(("row", "col"), None),
        P("row", "col", None, None, None),
        P("row", "col", None),
        P("row", "col", None),
        P(("row", "col")),
        P(),
        P(),
    )
    return jax.shard_map(
        per_device, mesh=mesh, in_specs=in_specs, out_specs=P(("row", "col"), None), check_vma=False)
```

```python
import jax
import jax.numpy as jnp
from jax import lax
from jax.experimental import pallas as pl
from jax.experimental.pallas import tpu as pltpu
from jax.sharding import PartitionSpec as P

MESH = pl.DeviceIdType.MESH
BS = 128
D = 256
PIECE = 512
NBLK = 736
LANES = 768
ROW_BLOCKS = 32
COL_BLOCKS = 64
UPPER = 224


def row_at(i, dz, dx, dc):
    return ((i // 8 + dz) % 2) * 8 + ((i // 2 + dx + 4) % 4) * 2 + (i + dc) % 2


def col_at(j, dz, dy):
    return ((j // 4 + dz) % 2) * 4 + (j + dy + 4) % 4


def gather_plan():
    upper, lower = (0, UPPER), (UPPER, PIECE - UPPER)
    first, second = (0, UPPER // 2), (UPPER // 2, UPPER // 2)
    rest = (PIECE - UPPER) // 2
    third, fourth = (UPPER, rest), (UPPER + rest, rest)
    right, left, over, core = (0, 1, 0), (0, -1, 0), (1, 0, 0), (0, 0, 1)
    return [
        (None, [
            ("a1", (0, 0), *upper, right), ("a2", (0, 0), *upper, left),
            ("bz", (0, 0), *lower, over), ("az", (0, 0), *upper, over),
            ("b1", (0, 0), *lower, right), ("b2", (0, 0), *lower, left),
            ("s0", (0, 0), 0, PIECE, core)]),
        ("a1", [("az1", (0, -1), *upper, over), ("a3", (0, -1), *first, right),
                ("s1", (0, -1), *upper, core)]),
        ("a2", [("az2", (0, 1), *upper, over), ("a4", (0, 1), *second, left),
                ("s2", (0, 1), *upper, core)]),
        ("bz", [("zb1", (1, 0), *lower, right), ("zb2", (1, 0), *lower, left),
                ("s3", (1, 0), *lower, core)]),
        ("b1", [("b3", (0, -1), *third, right), ("s4", (0, -1), *lower, core)]),
        ("b2", [("b4", (0, 1), *fourth, left), ("s5", (0, 1), *lower, core)]),
        ("az", [("s6", (1, 0), *upper, core)]),
        ("a3", [("az3", (0, 2), *first, over), ("s7", (0, 2), *first, core)]),
        ("a4", [("az4", (0, 2), *second, over), ("s8", (0, 2), *second, core)]),
        ("zb1", [("zb3", (1, -1), *third, right), ("s9", (1, -1), *lower, core)]),
        ("zb2", [("zb4", (1, 1), *fourth, left), ("s10", (1, 1), *lower, core)]),
        ("az1", [("s11", (1, -1), *upper, core)]),
        ("az2", [("s12", (1, 1), *upper, core)]),
        ("b3", [("s13", (0, 2), *third, core)]),
        ("b4", [("s14", (0, 2), *fourth, core)]),
        ("zb3", [("s15", (1, 2), *third, core)]),
        ("zb4", [("s16", (1, 2), *fourth, core)]),
        ("az3", [("s17", (1, 2), *first, core)]),
        ("az4", [("s18", (1, 2), *second, core)]),
    ]


PLAN = gather_plan()
SENDS = {copy[0]: copy for _, copies in PLAN for copy in copies}
PLACE = {name: k for k, name in enumerate(SENDS)}
PASSED_ON = [name for name, _ in PLAN]


PIECES = [(1, 2), (0, 2), (1, -1), (1, 1), (0, -1), (0, 1), (1, 0), (0, 0)]
WHOLE = [(piece, 0) for piece in PIECES]
HALVES = [
    ((1, 2), 0), ((1, 2), 2), ((0, 2), 2), ((1, -1), 0), ((1, -1), 2), ((1, 1), 0), ((1, 1), 2),
    ((0, 2), 0), ((1, 0), 0), ((0, -1), 2), ((0, 1), 2), ((1, 0), 2), ((0, -1), 0), ((0, 1), 0),
    ((0, 0), 0), ((0, 0), 2),
]
PROGRAM = [
    ([], WHOLE[:1], 4, {0: ("a1", "a2", "bz", "b1", "b2", "az")}),
    ([(0, 0), (0, 1), (0, -1)], WHOLE, 4, {
        0: ("a3", "a4"), 1: ("zb1", "zb2"), 2: ("az1", "az2"), 3: ("b3", "b4"),
        4: ("zb3", "zb4"), 5: ("az3", "az4")}),
    ([(1, 0), (0, 2), (1, 1), (1, -1), (1, 2)], HALVES, 2, {
        0: ("z2",), 1: ("o2r", "o2l"), 2: ("m2r", "m2l"), 3: ("zl",), 4: ("o1l",), 5: ("zr",),
        6: ("o1r",), 7: ("n2r", "n2l"), 8: ("o0z",), 9: ("m1l",), 10: ("m1r",), 11: ("o0y",),
        12: ("n1l",), 13: ("n1r",)}),
]
ZR, ZL, YL, YR = 0, 128, 256, 384
Z, Y, ALL = (ZR, YL), (YL, PIECE), (ZR, PIECE)
OVER, RIGHT, LEFT = (1, 0), (0, 1), (0, -1)
PARTS = {
    "z2": ((1, 2), Z, OVER, ()), "zl": ((1, -1), Z, OVER, ()), "zr": ((1, 1), Z, OVER, ()),
    "o2r": ((1, 2), (YR, PIECE), RIGHT, ()), "o2l": ((1, 2), (YL, YR), LEFT, ()),
    "o1r": ((1, 1), Y, RIGHT, ("o2r",)), "o1l": ((1, -1), Y, LEFT, ("o2l",)),
    "n2r": ((0, 2), (ZR, ZL), RIGHT, ("z2",)), "n2l": ((0, 2), (ZL, YL), LEFT, ("z2",)),
    "m2r": ((0, 2), (YR, PIECE), RIGHT, ()), "m2l": ((0, 2), (YL, YR), LEFT, ()),
    "n1r": ((0, 1), Z, RIGHT, ("zr", "n2r")), "n1l": ((0, -1), Z, LEFT, ("zl", "n2l")),
    "m1r": ((0, 1), Y, RIGHT, ("m2r",)), "m1l": ((0, -1), Y, LEFT, ("m2l",)),
    "o0z": ((1, 0), Z, OVER, ()), "o0y": ((1, 0), Y, OVER, ("o1r", "o1l")),
}
PART_PLACE = {name: k for k, name in enumerate(PARTS)}
PART_START = {}
PART_ROWS = 0
for _name, _part in PARTS.items():
    PART_START[_name] = PART_ROWS
    PART_ROWS += _part[1][1] - _part[1][0]


def kernel(
    rows_hbm, cols_hbm, degree_hbm, w_self_hbm, w_neigh_hbm, x_hbm, a_hbm, out_ref,
    gathered, blocks, table_v, table_s, own, acc, sent, got, slots,
    rows_v, cols_v, degree_v, shares, w_self, w_neigh,
    load_sem, table_sem, g_send, g_recv, c_send, c_recv,
):
    i, j = lax.axis_index("row"), lax.axis_index("col")

    loads = [
        pltpu.make_async_copy(source, target, load_sem.at[k])
        for k, (source, target) in enumerate([
            (rows_hbm, rows_v), (cols_hbm, cols_v), (x_hbm, gathered.at[i]), (w_self_hbm, w_self),
            (a_hbm, blocks.at[pl.ds(1, NBLK)]), (degree_hbm, degree_v), (w_neigh_hbm, w_neigh)])
    ]
    for load in loads:
        load.start()

    barrier = pltpu.get_barrier_semaphore()
    near = [(0, 1, 0), (0, -1, 0), (1, 0, 0), (0, 0, 1)]
    for offset in near:
        pl.semaphore_signal(barrier, inc=1, device_id=(row_at(i, *offset), j), device_id_type=MESH)
    for offset in (OVER, RIGHT, LEFT):
        pl.semaphore_signal(barrier, inc=1, device_id=(i, col_at(j, *offset)), device_id_type=MESH)
    pl.semaphore_wait(barrier, len(near) + 3)

    def gather_copy(name, arriving=False):
        _, (dz, dx), first, count, target = SENDS[name]
        if arriving:
            place = row_at(i, dz - target[0], dx - target[1], -target[2])
        else:
            place = row_at(i, dz, dx, 0)
        region = gathered.at[place, pl.ds(first, count)]
        source = region
        if not arriving and (dz, dx) == (0, 0):
            source = x_hbm.at[pl.ds(first, count)]
        return pltpu.make_async_remote_copy(
            src_ref=source, dst_ref=region,
            send_sem=g_send.at[PLACE[name]], recv_sem=g_recv.at[PLACE[name]],
            device_id=(row_at(i, *target), j), device_id_type=MESH)

    waited = set()

    def gather_wait(*names):
        for name in names:
            gather_copy(name, arriving=True).wait_recv()
            waited.add(name)

    def gather_steps(*names):
        for name, copies in PLAN:
            if name in names:
                if name is not None:
                    gather_wait(name)
                for copy in copies:
                    gather_copy(copy[0]).start()

    gather_steps(None)

    loads[0].wait()
    loads[1].wait()
    slots[...] = jnp.full_like(slots, -1)
    slots[0:1, 0:NBLK] = rows_v[...]
    slots[1:2, 0:NBLK] = cols_v[...]
    place = lax.broadcasted_iota(jnp.int32, (COL_BLOCKS, LANES), 1) + 1
    here = lax.broadcasted_iota(jnp.int32, (COL_BLOCKS, LANES), 0) == slots[1:2, :]
    in_row = lax.broadcasted_iota(jnp.int32, (ROW_BLOCKS, LANES), 0) == slots[0:1, :]
    in_row = in_row.astype(jnp.float32).astype(jnp.bfloat16)
    high = jnp.where(here, place >> 5, 0).astype(jnp.float32).astype(jnp.bfloat16)
    low = jnp.where(here, place & 31, 0).astype(jnp.float32).astype(jnp.bfloat16)
    dims = (((1,), (1,)), ((), ()))
    found = 32.0 * lax.dot_general(in_row, high, dims, preferred_element_type=jnp.float32)
    found += lax.dot_general(in_row, low, dims, preferred_element_type=jnp.float32)
    table_v[...] = jnp.clip(found.astype(jnp.int32), 0, NBLK)
    table_copy = pltpu.make_async_copy(table_v, table_s, table_sem)
    table_copy.start()
    blocks[0] = jnp.zeros((BS, BS), jnp.bfloat16)

    def clear(k, _):
        acc[k] = jnp.zeros((PIECE, D), jnp.float32)
        return 0

    lax.fori_loop(0, 8, clear, 0)
    loads[2].wait()
    loads[3].wait()
    for b in range(4):
        rows = pl.ds(b * BS, BS)
        own[rows, :] = jnp.dot(
            gathered[i, rows, :], w_self[...], preferred_element_type=jnp.float32)
    loads[5].wait()
    for b in range(4):
        degree = jnp.broadcast_to(degree_v[b:b + 1, :].astype(jnp.float32), (BS, BS)).T
        shares[b] = 1.0 / degree
    table_copy.wait()
    loads[4].wait()

    def add_products(piece, first, count, chips):
        for b in range(count):
            total = None
            for dz, dx in chips:
                chip = ((i // 8 + dz) % 2) * 4 + (i // 2 + dx + 4) % 4
                for c in range(0, 8, 2):
                    x = gathered[2 * chip + c // 4, pl.ds((c % 4) * BS, 2 * BS), :]
                    slot = [table_s[piece * 4 + first + b, chip * 8 + c + d] for d in range(2)]
                    a = jnp.concatenate([blocks[slot[0]], blocks[slot[1]]], axis=1)
                    term = jnp.dot(a, x, preferred_element_type=jnp.float32)
                    total = term if total is None else total + term
            acc[piece, pl.ds((first + b) * BS, BS), :] += total

    def part_copy(name):
        piece, (first, last), target, _ = PARTS[name]
        return pltpu.make_async_remote_copy(
            src_ref=sent.at[PIECES.index(piece), pl.ds(first, last - first)],
            dst_ref=got.at[pl.ds(PART_START[name], last - first)],
            send_sem=c_send.at[PART_PLACE[name]], recv_sem=c_recv.at[PART_PLACE[name]],
            device_id=(i, col_at(j, *target)), device_id_type=MESH)

    arrived = set()

    def add_arrived(value, names, first, last):
        for name in names:
            start, stop = PARTS[name][1]
            if start <= first and last <= stop:
                place = PART_START[name] + first - start
                value += got[pl.ds(place, last - first), :].astype(jnp.float32)
        return value

    def send_part(name):
        piece, (first, last), _, needs = PARTS[name]
        for need in needs:
            if need not in arrived:
                part_copy(need).wait_recv()
                arrived.add(need)
        cuts = {first, last}
        for need in needs:
            cuts |= {cut for cut in PARTS[need][1] if first < cut < last}
        cuts = sorted(cuts)
        for low, high in zip(cuts, cuts[1:]):
            value = acc[col_at(j, *piece), pl.ds(low, high - low), :]
            value = add_arrived(value, needs, low, high)
            sent[PIECES.index(piece), pl.ds(low, high - low), :] = value.astype(jnp.bfloat16)
        part_copy(name).start()

    def await_features(chip):
        for name, (_, (dz, dx), _, _, target) in SENDS.items():
            if ((dz - target[0]) % 2, (dx - target[1]) % 4) == (chip[0] % 2, chip[1] % 4):
                if name in waited:
                    continue
                gather_steps(name) if name in PASSED_ON else gather_wait(name)

    for chips, steps, count, actions in PROGRAM:
        for chip in chips:
            await_features(chip)

        for k, ((z, y), first) in enumerate(steps):
            if chips:
                add_products(col_at(j, z, y), first, count, chips)
            for name in actions.get(k, ()):
                send_part(name) if name in PARTS else gather_steps(name)

    loads[6].wait()
    for names, blocks_done in ((("m1l", "m1r", "o0y"), (2, 3)), (("o0z", "n1l", "n1r"), (0, 1))):
        for name in names:
            part_copy(name).wait_recv()
        for b in blocks_done:
            rows = pl.ds(b * BS, BS)
            total = add_arrived(acc[j, rows, :], names, b * BS, (b + 1) * BS)
            share = jnp.concatenate([shares[b], shares[b]], axis=1)
            mean = (total * share).astype(jnp.bfloat16)
            new = own[rows, :] + jnp.dot(mean, w_neigh[...], preferred_element_type=jnp.float32)
            out_ref[rows, :] = jnp.maximum(new, 0.0).astype(jnp.bfloat16)
    for name in PARTS:
        part_copy(name).wait_send()
    for name in SENDS:
        gather_copy(name).wait_send()


def per_device(features, weights, slot_row, slot_column, degree, w_self, w_neigh):
    hbm = pl.BlockSpec(memory_space=pltpu.HBM)
    count = len(SENDS)
    return pl.pallas_call(
        kernel,
        out_shape=jax.ShapeDtypeStruct((PIECE, D), jnp.bfloat16),
        in_specs=[hbm] * 7,
        out_specs=pl.BlockSpec(memory_space=pltpu.VMEM),
        scratch_shapes=[
            pltpu.VMEM((16, PIECE, D), jnp.bfloat16),
            pltpu.VMEM((NBLK + 1, BS, BS), jnp.bfloat16),
            pltpu.VMEM((ROW_BLOCKS, COL_BLOCKS), jnp.int32),
            pltpu.SMEM((ROW_BLOCKS, COL_BLOCKS), jnp.int32),
            pltpu.VMEM((PIECE, D), jnp.float32),
            pltpu.VMEM((8, PIECE, D), jnp.float32),
            pltpu.VMEM((7, PIECE, D), jnp.bfloat16),
            pltpu.VMEM((PART_ROWS, D), jnp.bfloat16),
            pltpu.VMEM((8, LANES), jnp.int32),
            pltpu.VMEM((1, NBLK), jnp.int32),
            pltpu.VMEM((1, NBLK), jnp.int32),
            pltpu.VMEM((4, BS), jnp.int32),
            pltpu.VMEM((4, BS, BS), jnp.float32),
            pltpu.VMEM((D, D), jnp.bfloat16),
            pltpu.VMEM((D, D), jnp.bfloat16),
            pltpu.SemaphoreType.DMA((7,)),
            pltpu.SemaphoreType.DMA,
            pltpu.SemaphoreType.DMA((count,)),
            pltpu.SemaphoreType.DMA((count,)),
            pltpu.SemaphoreType.DMA((len(PARTS),)),
            pltpu.SemaphoreType.DMA((len(PARTS),)),
        ],
        compiler_params=pltpu.CompilerParams(
            collective_id=0, has_side_effects=True, vmem_limit_bytes=52 * 2**20),
        name="sage_layer",
    )(*[
        pltpu.with_memory_space_constraint(operand, pltpu.HBM)
        for operand in (
            slot_row.reshape(1, NBLK), slot_column.reshape(1, NBLK), degree.reshape(4, BS),
            w_self, w_neigh, features, weights.reshape(NBLK, BS, BS))
    ])


def solution(mesh):
    in_specs = (
        P(("row", "col"), None),
        P("row", "col", None, None, None),
        P("row", "col", None),
        P("row", "col", None),
        P(("row", "col")),
        P(),
        P(),
    )
    return jax.shard_map(
        per_device, mesh=mesh, in_specs=in_specs, out_specs=P(("row", "col"), None), check_vma=False)
```

```python
import jax
import jax.numpy as jnp
from jax import lax
from jax.experimental import pallas as pl
from jax.experimental.pallas import tpu as pltpu
from jax.sharding import PartitionSpec as P

MESH = pl.DeviceIdType.MESH
BS = 128
D = 256
PIECE = 512
NBLK = 736
LANES = 768
ROW_BLOCKS = 32
COL_BLOCKS = 64
UPPER = 224


def row_at(i, dz, dx, dc):
    return ((i // 8 + dz) % 2) * 8 + ((i // 2 + dx + 4) % 4) * 2 + (i + dc) % 2


def col_at(j, dz, dy):
    return ((j // 4 + dz) % 2) * 4 + (j + dy + 4) % 4


def gather_plan():
    upper, lower = (0, UPPER), (UPPER, PIECE - UPPER)
    first, second = (0, UPPER // 2), (UPPER // 2, UPPER // 2)
    rest = (PIECE - UPPER) // 2
    third, fourth = (UPPER, rest), (UPPER + rest, rest)
    right, left, over, core = (0, 1, 0), (0, -1, 0), (1, 0, 0), (0, 0, 1)
    return [
        (None, [
            ("a1", (0, 0), *upper, right), ("a2", (0, 0), *upper, left),
            ("bz", (0, 0), *lower, over), ("az", (0, 0), *upper, over),
            ("b1", (0, 0), *lower, right), ("b2", (0, 0), *lower, left),
            ("s0", (0, 0), 0, PIECE, core)]),
        ("a1", [("az1", (0, -1), *upper, over), ("a3", (0, -1), *first, right),
                ("s1", (0, -1), *upper, core)]),
        ("a2", [("az2", (0, 1), *upper, over), ("a4", (0, 1), *second, left),
                ("s2", (0, 1), *upper, core)]),
        ("bz", [("zb1", (1, 0), *lower, right), ("zb2", (1, 0), *lower, left),
                ("s3", (1, 0), *lower, core)]),
        ("b1", [("b3", (0, -1), *third, right), ("s4", (0, -1), *lower, core)]),
        ("b2", [("b4", (0, 1), *fourth, left), ("s5", (0, 1), *lower, core)]),
        ("az", [("s6", (1, 0), *upper, core)]),
        ("a3", [("az3", (0, 2), *first, over), ("s7", (0, 2), *first, core)]),
        ("a4", [("az4", (0, 2), *second, over), ("s8", (0, 2), *second, core)]),
        ("zb1", [("zb3", (1, -1), *third, right), ("s9", (1, -1), *lower, core)]),
        ("zb2", [("zb4", (1, 1), *fourth, left), ("s10", (1, 1), *lower, core)]),
        ("az1", [("s11", (1, -1), *upper, core)]),
        ("az2", [("s12", (1, 1), *upper, core)]),
        ("b3", [("s13", (0, 2), *third, core)]),
        ("b4", [("s14", (0, 2), *fourth, core)]),
        ("zb3", [("s15", (1, 2), *third, core)]),
        ("zb4", [("s16", (1, 2), *fourth, core)]),
        ("az3", [("s17", (1, 2), *first, core)]),
        ("az4", [("s18", (1, 2), *second, core)]),
    ]


PLAN = gather_plan()
SENDS = {copy[0]: copy for _, copies in PLAN for copy in copies}
PLACE = {name: k for k, name in enumerate(SENDS)}
PASSED_ON = [name for name, _ in PLAN]


PIECES = [(1, 2), (0, 2), (1, -1), (1, 1), (0, -1), (0, 1), (1, 0), (0, 0)]
WHOLE = [(piece, 0) for piece in PIECES]
HALVES = [
    ((1, 2), 0), ((1, 2), 2), ((0, 2), 2), ((1, -1), 0), ((1, -1), 2), ((1, 1), 0), ((1, 1), 2),
    ((0, 2), 0), ((1, 0), 0), ((0, -1), 2), ((0, 1), 2), ((1, 0), 2), ((0, -1), 0), ((0, 1), 0),
    ((0, 0), 0), ((0, 0), 2),
]
PROGRAM = [
    ([], WHOLE[:1], 4, {0: ("a1", "a2", "bz", "b1", "b2", "az")}),
    ([(0, 0)], WHOLE, 4, {7: ("a3", "a4")}),
    ([(0, 1), (0, -1)], WHOLE, 4, {
        0: ("az1",), 2: ("zb1", "zb2"), 3: ("az2",), 4: ("b3", "b4"), 6: ("az3",),
        7: ("zb3", "zb4", "az4")}),
    ([(1, 0)], HALVES[:4], 2, {}),
    ([(0, 2), (1, 1), (1, -1), (1, 2)], HALVES[:4], 2, {0: ("z2",), 1: ("o2r", "o2l"), 2: ("m2r", "m2l"), 3: ("zl",)}),
    ([(1, 0), (0, 2), (1, 1), (1, -1), (1, 2)], HALVES[4:], 2, {1: ("zr", "o1l"), 2: ("o1r",), 3: ("n2r", "n2l"), 4: ("o0z",), 5: ("m1l",), 6: ("m1r",), 7: ("o0y",), 9: ("n1l",), 10: ("n1r",)}),
]
ZR, ZL, YL, YR = 0, 128, 256, 384
Z, Y, ALL = (ZR, YL), (YL, PIECE), (ZR, PIECE)
OVER, RIGHT, LEFT = (1, 0), (0, 1), (0, -1)
PARTS = {
    "z2": ((1, 2), Z, OVER, ()), "zl": ((1, -1), Z, OVER, ()), "zr": ((1, 1), Z, OVER, ()),
    "o2r": ((1, 2), (YR, PIECE), RIGHT, ()), "o2l": ((1, 2), (YL, YR), LEFT, ()),
    "o1r": ((1, 1), Y, RIGHT, ("o2r",)), "o1l": ((1, -1), Y, LEFT, ("o2l",)),
    "n2r": ((0, 2), (ZR, ZL), RIGHT, ("z2",)), "n2l": ((0, 2), (ZL, YL), LEFT, ("z2",)),
    "m2r": ((0, 2), (YR, PIECE), RIGHT, ()), "m2l": ((0, 2), (YL, YR), LEFT, ()),
    "n1r": ((0, 1), Z, RIGHT, ("zr", "n2r")), "n1l": ((0, -1), Z, LEFT, ("zl", "n2l")),
    "m1r": ((0, 1), Y, RIGHT, ("m2r",)), "m1l": ((0, -1), Y, LEFT, ("m2l",)),
    "o0z": ((1, 0), Z, OVER, ()), "o0y": ((1, 0), Y, OVER, ("o1r", "o1l")),
}
PART_PLACE = {name: k for k, name in enumerate(PARTS)}
PART_START = {}
PART_ROWS = 0
for _name, _part in PARTS.items():
    PART_START[_name] = PART_ROWS
    PART_ROWS += _part[1][1] - _part[1][0]


def kernel(
    rows_hbm, cols_hbm, degree_hbm, w_self_hbm, w_neigh_hbm, x_hbm, a_hbm, out_ref,
    gathered, blocks, table_v, table_s, own, acc, sent, got, slots,
    rows_v, cols_v, degree_v, shares, w_self, w_neigh,
    load_sem, table_sem, g_send, g_recv, c_send, c_recv,
):
    i, j = lax.axis_index("row"), lax.axis_index("col")

    loads = [
        pltpu.make_async_copy(source, target, load_sem.at[k])
        for k, (source, target) in enumerate([
            (rows_hbm, rows_v), (cols_hbm, cols_v), (x_hbm, gathered.at[i]), (w_self_hbm, w_self),
            (a_hbm, blocks.at[pl.ds(1, NBLK)]), (degree_hbm, degree_v), (w_neigh_hbm, w_neigh)])
    ]
    for load in loads:
        load.start()

    barrier = pltpu.get_barrier_semaphore()
    near = [(0, 1, 0), (0, -1, 0), (1, 0, 0), (0, 0, 1)]
    for offset in near:
        pl.semaphore_signal(barrier, inc=1, device_id=(row_at(i, *offset), j), device_id_type=MESH)
    for offset in (OVER, RIGHT, LEFT):
        pl.semaphore_signal(barrier, inc=1, device_id=(i, col_at(j, *offset)), device_id_type=MESH)
    pl.semaphore_wait(barrier, len(near) + 3)

    def gather_copy(name, arriving=False):
        _, (dz, dx), first, count, target = SENDS[name]
        if arriving:
            place = row_at(i, dz - target[0], dx - target[1], -target[2])
        else:
            place = row_at(i, dz, dx, 0)
        region = gathered.at[place, pl.ds(first, count)]
        source = region
        if not arriving and (dz, dx) == (0, 0):
            source = x_hbm.at[pl.ds(first, count)]
        return pltpu.make_async_remote_copy(
            src_ref=source, dst_ref=region,
            send_sem=g_send.at[PLACE[name]], recv_sem=g_recv.at[PLACE[name]],
            device_id=(row_at(i, *target), j), device_id_type=MESH)

    waited = set()

    def gather_wait(*names):
        for name in names:
            gather_copy(name, arriving=True).wait_recv()
            waited.add(name)

    def gather_steps(*names):
        for name, copies in PLAN:
            if name in names:
                if name is not None:
                    gather_wait(name)
                for copy in copies:
                    gather_copy(copy[0]).start()

    gather_steps(None)

    loads[0].wait()
    loads[1].wait()
    slots[...] = jnp.full_like(slots, -1)
    slots[0:1, 0:NBLK] = rows_v[...]
    slots[1:2, 0:NBLK] = cols_v[...]
    place = lax.broadcasted_iota(jnp.int32, (COL_BLOCKS, LANES), 1) + 1
    here = lax.broadcasted_iota(jnp.int32, (COL_BLOCKS, LANES), 0) == slots[1:2, :]
    in_row = lax.broadcasted_iota(jnp.int32, (ROW_BLOCKS, LANES), 0) == slots[0:1, :]
    in_row = in_row.astype(jnp.float32).astype(jnp.bfloat16)
    high = jnp.where(here, place >> 5, 0).astype(jnp.float32).astype(jnp.bfloat16)
    low = jnp.where(here, place & 31, 0).astype(jnp.float32).astype(jnp.bfloat16)
    dims = (((1,), (1,)), ((), ()))
    found = 32.0 * lax.dot_general(in_row, high, dims, preferred_element_type=jnp.float32)
    found += lax.dot_general(in_row, low, dims, preferred_element_type=jnp.float32)
    table_v[...] = jnp.clip(found.astype(jnp.int32), 0, NBLK)
    table_copy = pltpu.make_async_copy(table_v, table_s, table_sem)
    table_copy.start()
    blocks[0] = jnp.zeros((BS, BS), jnp.bfloat16)

    def clear(k, _):
        acc[k] = jnp.zeros((PIECE, D), jnp.float32)
        return 0

    lax.fori_loop(0, 8, clear, 0)
    loads[2].wait()
    loads[3].wait()
    for b in range(4):
        rows = pl.ds(b * BS, BS)
        own[rows, :] = jnp.dot(
            gathered[i, rows, :], w_self[...], preferred_element_type=jnp.float32)
    loads[5].wait()
    for b in range(4):
        degree = jnp.broadcast_to(degree_v[b:b + 1, :].astype(jnp.float32), (BS, BS)).T
        shares[b] = 1.0 / degree
    table_copy.wait()
    loads[4].wait()

    def add_products(piece, first, count, chips):
        for b in range(count):
            total = None
            for dz, dx in chips:
                chip = ((i // 8 + dz) % 2) * 4 + (i // 2 + dx + 4) % 4
                for c in range(0, 8, 2):
                    x = gathered[2 * chip + c // 4, pl.ds((c % 4) * BS, 2 * BS), :]
                    slot = [table_s[piece * 4 + first + b, chip * 8 + c + d] for d in range(2)]
                    a = jnp.concatenate([blocks[slot[0]], blocks[slot[1]]], axis=1)
                    term = jnp.dot(a, x, preferred_element_type=jnp.float32)
                    total = term if total is None else total + term
            acc[piece, pl.ds((first + b) * BS, BS), :] += total

    def part_copy(name):
        piece, (first, last), target, _ = PARTS[name]
        return pltpu.make_async_remote_copy(
            src_ref=sent.at[PIECES.index(piece), pl.ds(first, last - first)],
            dst_ref=got.at[pl.ds(PART_START[name], last - first)],
            send_sem=c_send.at[PART_PLACE[name]], recv_sem=c_recv.at[PART_PLACE[name]],
            device_id=(i, col_at(j, *target)), device_id_type=MESH)

    arrived = set()

    def add_arrived(value, names, first, last):
        for name in names:
            start, stop = PARTS[name][1]
            if start <= first and last <= stop:
                place = PART_START[name] + first - start
                value += got[pl.ds(place, last - first), :].astype(jnp.float32)
        return value

    def send_part(name):
        piece, (first, last), _, needs = PARTS[name]
        for need in needs:
            if need not in arrived:
                part_copy(need).wait_recv()
                arrived.add(need)
        cuts = {first, last}
        for need in needs:
            cuts |= {cut for cut in PARTS[need][1] if first < cut < last}
        cuts = sorted(cuts)
        for low, high in zip(cuts, cuts[1:]):
            value = acc[col_at(j, *piece), pl.ds(low, high - low), :]
            value = add_arrived(value, needs, low, high)
            sent[PIECES.index(piece), pl.ds(low, high - low), :] = value.astype(jnp.bfloat16)
        part_copy(name).start()

    def await_features(chip):
        for name, (_, (dz, dx), _, _, target) in SENDS.items():
            if ((dz - target[0]) % 2, (dx - target[1]) % 4) == (chip[0] % 2, chip[1] % 4):
                if name in waited:
                    continue
                gather_steps(name) if name in PASSED_ON else gather_wait(name)

    for chips, steps, count, actions in PROGRAM:
        for chip in chips:
            await_features(chip)

        for k, ((z, y), first) in enumerate(steps):
            if chips:
                add_products(col_at(j, z, y), first, count, chips)
            for name in actions.get(k, ()):
                send_part(name) if name in PARTS else gather_steps(name)

    loads[6].wait()
    for names, blocks_done in ((("m1l", "m1r", "o0y"), (2, 3)), (("o0z", "n1l", "n1r"), (0, 1))):
        for name in names:
            part_copy(name).wait_recv()
        for b in blocks_done:
            rows = pl.ds(b * BS, BS)
            total = add_arrived(acc[j, rows, :], names, b * BS, (b + 1) * BS)
            share = jnp.concatenate([shares[b], shares[b]], axis=1)
            mean = (total * share).astype(jnp.bfloat16)
            new = own[rows, :] + jnp.dot(mean, w_neigh[...], preferred_element_type=jnp.float32)
            out_ref[rows, :] = jnp.maximum(new, 0.0).astype(jnp.bfloat16)
    for name in PARTS:
        part_copy(name).wait_send()
    for name in SENDS:
        gather_copy(name).wait_send()


def per_device(features, weights, slot_row, slot_column, degree, w_self, w_neigh):
    hbm = pl.BlockSpec(memory_space=pltpu.HBM)
    count = len(SENDS)
    return pl.pallas_call(
        kernel,
        out_shape=jax.ShapeDtypeStruct((PIECE, D), jnp.bfloat16),
        in_specs=[hbm] * 7,
        out_specs=pl.BlockSpec(memory_space=pltpu.VMEM),
        scratch_shapes=[
            pltpu.VMEM((16, PIECE, D), jnp.bfloat16),
            pltpu.VMEM((NBLK + 1, BS, BS), jnp.bfloat16),
            pltpu.VMEM((ROW_BLOCKS, COL_BLOCKS), jnp.int32),
            pltpu.SMEM((ROW_BLOCKS, COL_BLOCKS), jnp.int32),
            pltpu.VMEM((PIECE, D), jnp.float32),
            pltpu.VMEM((8, PIECE, D), jnp.float32),
            pltpu.VMEM((7, PIECE, D), jnp.bfloat16),
            pltpu.VMEM((PART_ROWS, D), jnp.bfloat16),
            pltpu.VMEM((8, LANES), jnp.int32),
            pltpu.VMEM((1, NBLK), jnp.int32),
            pltpu.VMEM((1, NBLK), jnp.int32),
            pltpu.VMEM((4, BS), jnp.int32),
            pltpu.VMEM((4, BS, BS), jnp.float32),
            pltpu.VMEM((D, D), jnp.bfloat16),
            pltpu.VMEM((D, D), jnp.bfloat16),
            pltpu.SemaphoreType.DMA((7,)),
            pltpu.SemaphoreType.DMA,
            pltpu.SemaphoreType.DMA((count,)),
            pltpu.SemaphoreType.DMA((count,)),
            pltpu.SemaphoreType.DMA((len(PARTS),)),
            pltpu.SemaphoreType.DMA((len(PARTS),)),
        ],
        compiler_params=pltpu.CompilerParams(
            collective_id=0, has_side_effects=True, vmem_limit_bytes=52 * 2**20),
        name="sage_layer",
    )(*[
        pltpu.with_memory_space_constraint(operand, pltpu.HBM)
        for operand in (
            slot_row.reshape(1, NBLK), slot_column.reshape(1, NBLK), degree.reshape(4, BS),
            w_self, w_neigh, features, weights.reshape(NBLK, BS, BS))
    ])


def solution(mesh):
    in_specs = (
        P(("row", "col"), None),
        P("row", "col", None, None, None),
        P("row", "col", None),
        P("row", "col", None),
        P(("row", "col")),
        P(),
        P(),
    )
    return jax.shard_map(
        per_device, mesh=mesh, in_specs=in_specs, out_specs=P(("row", "col"), None), check_vma=False)
```
